256 devices in a mesh: wide: 32 (over z, x), narrow: 8 (over y, core).
Axes of the slice: x: 4, y: 4, z: 8, core: 2. Of those that a mesh axis runs over, the one named last changes fastest.
Arguments:
- factor: float32 [131072, 256], P(('wide', 'narrow')), may hold values from -1.5 to 1.5
- quant: bfloat16 [1024, 8, 4, 128, 128], P('wide', 'narrow'), may hold values from -3 to 3
- pattern: int32 [1024, 8, 4], P('wide', 'narrow'), may hold values from 0 to 127, as said below
- exponent: int32 [1024, 8, 4], P('wide', 'narrow'), may hold values from -3 to 1
Outputs:
- stepped: float32 [131072, 256], P(('wide', 'narrow'))
The draws below stay inside these ranges and needn't reach their ends.
Inputs may be any that keep to these rules, and one draw needn't show every extreme that they name: `pattern`: the 4 column blocks of one block row within one column slab are distinct. Block rows w * 4 * 8 to (w + 1) * 4 * 8 - 1 taken with one column slab n touch, among the column blocks c of that slab with equal c // 4, at most 2 distinct ones, and exactly 2 for some such group.
All inputs are finite; a program needn't handle non-finite values.
Results may differ from the reference program's by a relative error of at most 0.0037.
Values may be sent and summed in bfloat16 or wider, within the bound.
A program may use at most 192 MiB of HBM per device.

```python
import jax
import jax.numpy as jnp
from jax import lax

TILE = 128
RANK = 256
BLK_DEV = 4
CAP = 2
TPS = 4
SLAB = 128
NBR = 1024
NROWS = 131072
N_NARROW = 8


def draw_pattern(key, part):
    key = jax.random.fold_in(key, 11)
    owners = SLAB // BLK_DEV
    groups = NBR // SLAB
    rows_each = NBR // owners
    choices_each = owners * CAP
    key_offset, key_score = jax.random.split(key)
    offset = jax.random.randint(key_offset, (owners, groups, owners), 0, BLK_DEV)
    scores = jax.random.randint(key_score, (owners, rows_each, groups, choices_each), 0, 1 << 20)
    scores = scores * choices_each + jnp.arange(choices_each, dtype=jnp.int32)
    forced = (jnp.arange(rows_each, dtype=jnp.int32) == 0)[None, :, None, None] & (jnp.arange(choices_each, dtype=jnp.int32) < CAP)[None, None, None, :]
    scores = jnp.where(forced, scores - (1 << 20) * choices_each - choices_each, scores)
    order = jnp.argsort(scores, axis=-1)[..., :TPS].astype(jnp.int32)
    owner = order // CAP
    within = order % CAP
    spread = jnp.broadcast_to(offset[:, None, :, :], (owners, rows_each, groups, owners))
    start = jnp.take_along_axis(spread, owner, axis=-1)
    local = (start + within) % BLK_DEV
    pattern = owner * BLK_DEV + local
    return pattern.reshape(NBR, groups, TPS).astype(jnp.int32)


def place_ends(entries, stream_key, low, top_value):
    longest = entries.shape.index(max(entries.shape))
    spots = []
    for shift in (0, 1):
        where = [jax.random.randint(jax.random.fold_in(stream_key, axis), (), 0, length) for axis, length in enumerate(entries.shape)]
        where[longest] = (where[longest] + shift) % entries.shape[longest]
        spots.append(tuple(where))
    return entries.at[spots[0]].set(low).at[spots[1]].set(top_value)


def block_scale(rng, extent, shards, least, high):
    factor_of, own = 1.0, jax.random.fold_in(rng, 6)
    for dim, shards_of in shards:
        heights = jnp.exp(jax.random.uniform(jax.random.fold_in(own, dim), (shards_of,), jnp.float32, least / len(shards), high / len(shards)))
        factor_of = factor_of * jnp.repeat(heights, extent[dim] // shards_of).reshape([-1 if axis == dim else 1 for axis in range(len(extent))])
    return factor_of


def normal_values(rng, dims, scale, reach, pieces=(), kind=jnp.bfloat16):
    level = block_scale(rng, dims, pieces, -0.22, 0.18) if pieces else 1.0
    drawn = jax.random.normal(rng, dims, jnp.float32) * scale * level
    return jnp.minimum(jnp.maximum(drawn, -reach), reach).astype(kind)


def setup_inputs(seed: int = 0) -> dict:
    splits = jax.random.split(jax.random.key(seed), 5)
    factor = normal_values(splits[0], (NROWS, RANK), 0.25, 1.5, ((0, 256),), jnp.float32)
    quant = normal_values(splits[1], (NBR, N_NARROW, TPS, TILE, TILE), 0.5, 3.0, ((0, 32), (1, 8)))
    pattern = draw_pattern(jax.random.fold_in(splits[4], 71), 0)
    exponent = place_ends(jax.random.randint(splits[3], (NBR, N_NARROW, TPS), -3, 2), jax.random.fold_in(splits[3], 1), -3, 1).astype(jnp.int32)
    return dict(factor=factor, quant=quant, pattern=pattern, exponent=exponent)


step_rate = 0.01


def reference(factor, quant, pattern, exponent):
    tile_size = quant.shape[-1]
    rank_width = factor.shape[1]
    block_count = factor.shape[0] // tile_size
    compact = factor.astype(jnp.bfloat16)
    widened = lax.optimization_barrier(compact).astype(jnp.float32)
    blocks = widened.reshape(block_count, tile_size, rank_width)
    slab_ids = jnp.arange(N_NARROW, dtype=jnp.int32)[None, :, None]
    global_ids = ((pattern // BLK_DEV) * N_NARROW + slab_ids) * BLK_DEV + pattern % BLK_DEV
    global_ids = global_ids.astype(jnp.int32)

    def advance(carry, inputs):
        row_block, quant_row, expo_row, global_row = inputs
        columns = blocks[global_row]
        predicted = jnp.einsum("ir,ntjr->ntij", row_block, columns)
        scaled = quant_row.astype(jnp.float32) * jnp.exp2(expo_row.astype(jnp.float32))[:, :, None, None]
        misfit = (predicted - scaled).astype(jnp.bfloat16)
        misfit_wide = lax.optimization_barrier(misfit).astype(jnp.float32)
        row_term = jnp.einsum("ntij,ntjr->ir", misfit_wide, columns)
        column_term = jnp.einsum("ntij,ir->ntjr", misfit_wide, row_block)
        carry = carry.at[global_row.reshape(-1)].add(column_term.reshape(-1, tile_size, rank_width))
        return carry, row_term

    start = jnp.zeros((block_count, tile_size, rank_width), jnp.float32)
    column_grad, row_grad = lax.scan(advance, start, (blocks, quant, exponent, global_ids))
    total_grad = row_grad.reshape(-1, rank_width) + column_grad.reshape(-1, rank_width)
    return factor - step_rate * total_grad
```

```python
import jax
import jax.numpy as jnp
from jax import lax
from jax.experimental import pallas as pl
from jax.experimental.pallas import tpu as pltpu
from jax.sharding import PartitionSpec as P

step_rate = 0.01

MESH = pl.DeviceIdType.MESH
NX = 4
NZ = 8
NY = 4
NC = 2
BLK = 4
TILE = 128
RANK = 256
GROUP = 32
SLOTS = 64
HALF = 64
NONE = 128
FAR_FIRST = (4, 3, 5, 2, 6, 1, 7, 0)
BF = jnp.bfloat16
F32 = jnp.float32


def index_rows(pattern):
    lane32 = lax.broadcasted_iota(jnp.int32, (GROUP, TILE), 1)
    sub32 = lax.broadcasted_iota(jnp.int32, (GROUP, TILE), 0)
    spread = jnp.zeros((GROUP, TILE), jnp.int32)
    for t in range(4):
        spread = jnp.where((lane32 & 3) == t, jnp.broadcast_to(pattern[:, t : t + 1], (GROUP, TILE)), spread)
    flat = jnp.sum(jnp.where(sub32 == (lane32 >> 2), spread, 0), axis=0, keepdims=True)
    full = (TILE, TILE)
    lane = lax.broadcasted_iota(jnp.int32, full, 1)
    sub = lax.broadcasted_iota(jnp.int32, full, 0)
    across = jnp.broadcast_to(flat, full)
    down = across.T
    prev = jnp.max(jnp.where((across == down) & (sub < lane), sub, -1), axis=0, keepdims=True)
    prev = jnp.where(prev < 0, NONE, prev)
    held_down = jnp.max(jnp.where(across == sub, 1, 0), axis=1, keepdims=True)
    held_across = jnp.max(jnp.where(down == lane, 1, 0), axis=0, keepdims=True)
    before = ((lane >> 2) == (sub >> 2)) & (lane < sub)
    rank = jnp.sum(jnp.where(before, jnp.broadcast_to(held_across, full), 0), axis=1, keepdims=True)
    place = (sub >> 2) * 2 + jnp.broadcast_to(rank, full)
    slot = jnp.sum(jnp.where(across == sub, place, 0), axis=0, keepdims=True)
    wanted = (jnp.broadcast_to(held_down, full) == 1) & (place == lane)
    need = jnp.sum(jnp.where(wanted, sub & 3, 0), axis=0, keepdims=True)
    slot_down = jnp.broadcast_to(slot, full).T
    last = jnp.max(jnp.where(slot_down == lane, sub, -1), axis=0, keepdims=True)
    last = jnp.where(last < 0, NONE, last)
    return slot, prev, last, need


def kernel(
    pattern_ref, expo_ref, fac, quant_hbm, out_ref,
    qraw, qs0, qs1, rowp, panel0, panel1, sums, racc, rsend, rrecv,
    xs0, xs1, cs0, cs1, cr0, cr1, co0, co1, zs0, zs1, zr0, zr1, zown,
    idxv, idxs, nrv, nrs,
    *rest,
):
    zb = (rest[0:8], rest[8:16])
    qsem, isem, n_s, n_r, row_s, row_r, ring_s, ring_r, x_s, x_r, c_s, c_r, z_s, z_r, rr_s, rr_r = rest[16:]
    qs, panel, xs, cs, cr, co, zs, zr = (
        (qs0, qs1), (panel0, panel1), (xs0, xs1), (cs0, cs1), (cr0, cr1), (co0, co1), (zs0, zs1), (zr0, zr1)
    )
    w = lax.axis_index("wide")
    n = lax.axis_index("narrow")
    x, z = lax.rem(w, NX), lax.div(w, NX)
    y, c = lax.div(n, NC), lax.rem(n, NC)

    def x_peer(dx):
        return (z * NX + lax.rem(x + dx, NX), n)

    def z_peer(dz):
        return (lax.rem(z + dz, NZ) * NX + x, n)

    narrow_steps = [(dy, dc) for dy in range(NY) for dc in range(NC) if (dy, dc) != (0, 0)]

    def n_peer(dy, dc):
        return lax.rem(y + dy, NY) * NC + lax.rem(c + dc, NC)

    barrier = pltpu.get_barrier_semaphore()
    peers = [x_peer(d) for d in range(1, NX)] + [z_peer(d) for d in range(1, NZ)]
    peers += [(w, n_peer(*s)) for s in narrow_steps]
    for peer in peers:
        pl.semaphore_signal(barrier, inc=1, device_id=peer, device_id_type=MESH)

    fetch = pltpu.make_async_copy(quant_hbm, qraw, qsem)
    fetch.start()

    rows = index_rows(pattern_ref[...])
    idxv[...] = jnp.zeros((8, TILE), jnp.int32)
    for i, row in enumerate(rows):
        idxv[i : i + 1, :] = row
    spill = pltpu.make_async_copy(idxv, idxs, isem.at[0])
    spill.start()
    for k in range(BLK):
        block = fac[k * TILE : (k + 1) * TILE, :].astype(BF)
        rowp[n * BLK + k] = block
        zb[0][0][k] = block[:HALF]
        zb[1][0][k] = block[HALF:]
    sums[NONE] = jnp.zeros((HALF, RANK), F32)

    pl.semaphore_wait(barrier, len(peers))
    waits = []

    def send(src, dst, s_sem, r_sem, peer):
        copy = pltpu.make_async_remote_copy(
            src_ref=src, dst_ref=dst, send_sem=s_sem, recv_sem=r_sem, device_id=peer, device_id_type=MESH
        )
        copy.start()
        waits.append(copy)
        return copy

    needs = [send(idxv, nrv.at[dx - 1], n_s.at[dx - 1], n_r.at[dx - 1], x_peer(dx)) for dx in range(1, NX)]

    ring = {}

    def ring_send(h, r):
        up_src, up_dst = zb[h][(1 - r) % NZ], zb[h][(-r) % NZ]
        down_src, down_dst = zb[h][r - 1], zb[h][r]
        if r == 4:
            up_src, up_dst = up_src.at[pl.ds(0, 2)], up_dst.at[pl.ds(0, 2)]
            down_src, down_dst = down_src.at[pl.ds(2, 2)], down_dst.at[pl.ds(2, 2)]
        ring[h, r] = (
            send(up_src, up_dst, ring_s.at[h, 0, r - 1], ring_r.at[h, 0, r - 1], z_peer(1)),
            send(down_src, down_dst, ring_s.at[h, 1, r - 1], ring_r.at[h, 1, r - 1], z_peer(NZ - 1)),
        )

    ring_send(0, 1)
    mine = rowp.at[pl.ds(n * BLK, BLK)]
    row_in = [
        send(mine, mine, row_s.at[j], row_r.at[j], (w, n_peer(*s))) for j, s in enumerate(narrow_steps)
    ]
    ring_send(1, 1)

    spill.wait()
    for copy in needs:
        copy.wait_recv()
    spill = pltpu.make_async_copy(nrv, nrs, isem.at[1])
    spill.start()
    spill.wait()

    def owner(d, dx=0):
        return lax.rem(z + d, NZ) * NX + lax.rem(x + dx, NX)

    x_in = {0: [], 1: []}

    def spread_source(h, d):
        source = zb[h][d]
        at = owner(d) * 2
        for dx in (2, 1, 3):
            for r in range(2):
                xs[h][dx - 1, d, r] = source[nrs[NX - 1 - dx, 3, at + r]]
            x_in[h].append(
                send(
                    xs[h].at[dx - 1, d], panel[h].at[pl.ds(at, 2)],
                    x_s.at[h, dx - 1, d], x_r.at[h, dx - 1, d], x_peer(dx),
                )
            )
        for r in range(2):
            panel[h][at + r] = source[idxs[3, at + r]]

    for h in range(2):
        spread_source(h, 0)
        for r in range(1, 5):
            for copy in ring[h, r]:
                copy.wait_recv()
            if r < 4:
                ring_send(h, r + 1)
            spread_source(h, (-r) % NZ)
            if r < 4:
                spread_source(h, r)

    fetch.wait()
    low = lax.broadcasted_iota(jnp.int32, (TILE, TILE), 1) < HALF

    def scale_row(b, carry):
        for pair in range(2):
            parts = []
            for t in (2 * pair, 2 * pair + 1):
                grow = lax.shift_left(1, expo_ref[b, t] + 3).astype(F32) * 0.125
                parts.append(qraw[b, 0, t].astype(F32) * grow)
            a, b2 = parts
            qs0[b, pair] = jnp.where(low, a, pltpu.roll(b2, HALF, 1)).astype(BF)
            qs1[b, pair] = jnp.where(low, pltpu.roll(a, HALF, 1), b2).astype(BF)
        return carry

    lax.fori_loop(0, GROUP, scale_row, 0)

    for copy in row_in:
        copy.wait_recv()

    def compute(h):
        def step(b, carry):
            mine = rowp[b]
            cols = jnp.concatenate([panel[h][idxs[0, b * 4 + t]] for t in range(4)], axis=0)
            pred = lax.dot_general(mine, cols, (((1,), (1,)), ((), ())), preferred_element_type=F32)
            scaled = jnp.concatenate([qs[h][b, 0], qs[h][b, 1]], axis=1).astype(F32)
            misfit = (pred - scaled).astype(BF)
            row = jnp.dot(misfit, cols, preferred_element_type=F32)
            if h == 0:
                racc[b] = row
            else:
                row = row + racc[b]
                racc[b] = row
                rsend[b] = row.astype(BF)
            term = lax.dot_general(misfit, mine, (((0,), (0,)), ((), ())), preferred_element_type=F32)
            for t in range(4):
                i = b * 4 + t
                sums[i] = term[t * HALF : (t + 1) * HALF] + sums[idxs[1, i]]
            return carry

        lax.fori_loop(0, GROUP, step, 0)

    c_in = {}

    def send_terms(h):
        for d in FAR_FIRST:
            for dx in (2, 1, 3):
                at = owner(d, dx) * 2
                for r in range(2):
                    cs[h][dx - 1, d, r] = sums[idxs[2, at + r]].astype(BF)
                c_in[h, d, dx] = send(
                    cs[h].at[dx - 1, d], cr[h].at[dx - 1, d],
                    c_s.at[h, dx - 1, d], c_r.at[h, dx - 1, d], x_peer(dx),
                )
            at = owner(d) * 2
            for r in range(2):
                co[h][d, r] = sums[idxs[2, at + r]]

    for copy in x_in[0]:
        copy.wait_recv()
    compute(0)
    send_terms(0)
    for copy in x_in[1]:
        copy.wait_recv()
    compute(1)
    r_in = [
        send(
            rsend.at[pl.ds(n_peer(*s) * BLK, BLK)], rrecv.at[j], rr_s.at[j], rr_r.at[j], (w, n_peer(*s))
        )
        for j, s in enumerate(narrow_steps)
    ]
    send_terms(1)

    z_in = []
    for h in range(2):
        for d in FAR_FIRST:
            for dx in range(1, NX):
                c_in[h, d, dx].wait_recv()
            at = owner(d) * 2
            marks = []
            for source in range(4):
                for r in range(2):
                    place = idxs[3, at + r] if source == 3 else nrs[source, 3, at + r]
                    marks.append([jnp.where(place == k, 1.0, 0.0).astype(F32) for k in range(BLK)])

            def strip(i, carry, h=h, d=d, marks=marks):
                span = pl.ds(pl.multiple_of(i * 16, 16), 16)
                terms = []
                for source in range(4):
                    for r in range(2):
                        if source == 3:
                            terms.append(co[h][d, r, span, :])
                        else:
                            terms.append(cr[h][source, d, r, span, :].astype(F32))
                for k in range(BLK):
                    total = terms[0] * marks[0][k]
                    for term, mark in zip(terms[1:], marks[1:]):
                        total = total + term * mark[k]
                    if d == 0:
                        zown[h, k, span, :] = total
                    else:
                        zs[h][d - 1, k, span, :] = total.astype(BF)
                return carry

            lax.fori_loop(0, HALF // 16, strip, 0)
            if d != 0:
                z_in.append(
                    send(zs[h].at[d - 1], zr[h].at[d - 1], z_s.at[h, d - 1], z_r.at[h, d - 1], z_peer(d))
                )

    for copy in r_in:
        copy.wait_recv()
    for copy in z_in:
        copy.wait_recv()
    for h in range(2):
        for k in range(BLK):
            def finish(i, carry, h=h, k=k):
                span = pl.ds(pl.multiple_of(i * 16, 16), 16)
                inner = pl.ds(pl.multiple_of(h * HALF + i * 16, 16), 16)
                outer = pl.ds(pl.multiple_of(k * TILE + h * HALF + i * 16, 16), 16)
                total = zown[h, k, span, :] + racc[n * BLK + k, inner, :]
                for j in range(7):
                    total = total + zr[h][j, k, span, :].astype(F32)
                    total = total + rrecv[j, k, inner, :].astype(F32)
                out_ref[outer, :] = fac[outer, :] - step_rate * total
                return carry

            lax.fori_loop(0, HALF // 16, finish, 0)
    for copy in waits:
        copy.wait_send()


def body(factor, quant, pattern, exponent):
    vmem = pl.BlockSpec(memory_space=pltpu.VMEM)
    smem = pl.BlockSpec(memory_space=pltpu.SMEM)
    dma = pltpu.SemaphoreType.DMA
    V = pltpu.VMEM
    scratch = [
        V((GROUP, 1, 4, TILE, TILE), BF),
        V((GROUP, 2, TILE, TILE), BF), V((GROUP, 2, TILE, TILE), BF),
        V((GROUP, TILE, RANK), BF),
        V((SLOTS, HALF, RANK), BF), V((SLOTS, HALF, RANK), BF),
        V((NONE + 1, HALF, RANK), F32),
        V((GROUP, TILE, RANK), F32),
        V((GROUP, TILE, RANK), BF),
        V((7, BLK, TILE, RANK), BF),
    ]
    scratch += [V((3, NZ, 2, HALF, RANK), BF)] * 6
    scratch += [V((NZ, 2, HALF, RANK), F32)] * 2
    scratch += [V((7, BLK, HALF, RANK), BF)] * 4
    scratch += [V((2, BLK, HALF, RANK), F32)]
    scratch += [
        V((8, TILE), jnp.int32), pltpu.SMEM((8, TILE), jnp.int32),
        V((3, 8, TILE), jnp.int32), pltpu.SMEM((3, 8, TILE), jnp.int32),
    ]
    scratch += [V((BLK, HALF, RANK), BF)] * 16
    scratch += [
        dma, dma((2,)), dma((3,)), dma((3,)), dma((7,)), dma((7,)), dma((2, 2, 4)), dma((2, 2, 4)),
        dma((2, 3, NZ)), dma((2, 3, NZ)), dma((2, 3, NZ)), dma((2, 3, NZ)), dma((2, 7)), dma((2, 7)),
        dma((7,)), dma((7,)),
    ]
    return pl.pallas_call(
        kernel,
        out_shape=jax.ShapeDtypeStruct(factor.shape, factor.dtype),
        in_specs=[vmem, smem, vmem, pl.BlockSpec(memory_space=pl.ANY)],
        out_specs=vmem,
        scratch_shapes=scratch,
        compiler_params=pltpu.CompilerParams(
            collective_id=0, has_side_effects=True, vmem_limit_bytes=58 * 1024 * 1024
        ),
        cost_estimate=pl.CostEstimate(flops=3_300_000_000, bytes_accessed=6_000_000, transcendentals=0),
        name="completion_step",
    )(pattern[:, 0, :], exponent[:, 0, :], factor, quant)


def solution(mesh):
    in_specs = (
        P(("wide", "narrow"), None),
        P("wide", "narrow", None, None, None),
        P("wide", "narrow", None),
        P("wide", "narrow", None),
    )
    out_specs = P(("wide", "narrow"), None)
    return jax.shard_map(body, mesh=mesh, in_specs=in_specs, out_specs=out_specs, check_vma=False)
```

```python
import jax
import jax.numpy as jnp
from jax import lax
from jax.experimental import pallas as pl
from jax.experimental.pallas import tpu as pltpu
from jax.sharding import PartitionSpec as P

step_rate = 0.01

MESH = pl.DeviceIdType.MESH
NX = 4
NZ = 8
NY = 4
NC = 2
BLK = 4
TILE = 128
RANK = 256
GROUP = 32
SLOTS = 64
HALF = 64
NONE = 128
FAR_FIRST = (4, 3, 5, 2, 6, 1, 7, 0)
OVER_Z = {1: (1, 7), 2: (1, 7, 2, 6), 3: (1, 7)}
NEAR_Z = (1, 7, 2, 6)
MESSAGES = 160
LATE = 4
RING1, DENSE1, ZS = 2, 4, 3
BF = jnp.bfloat16
F32 = jnp.float32


def index_rows(pattern):
    lane32 = lax.broadcasted_iota(jnp.int32, (GROUP, TILE), 1)
    sub32 = lax.broadcasted_iota(jnp.int32, (GROUP, TILE), 0)
    spread = jnp.zeros((GROUP, TILE), jnp.int32)
    for t in range(4):
        spread = jnp.where((lane32 & 3) == t, jnp.broadcast_to(pattern[:, t : t + 1], (GROUP, TILE)), spread)
    flat = jnp.sum(jnp.where(sub32 == (lane32 >> 2), spread, 0), axis=0, keepdims=True)
    full = (TILE, TILE)
    lane = lax.broadcasted_iota(jnp.int32, full, 1)
    sub = lax.broadcasted_iota(jnp.int32, full, 0)
    across = jnp.broadcast_to(flat, full)
    down = across.T
    prev = jnp.max(jnp.where((across == down) & (sub < lane), sub, -1), axis=0, keepdims=True)
    prev = jnp.where(prev < 0, NONE, prev)
    held_down = jnp.max(jnp.where(across == sub, 1, 0), axis=1, keepdims=True)
    held_across = jnp.max(jnp.where(down == lane, 1, 0), axis=0, keepdims=True)
    before = ((lane >> 2) == (sub >> 2)) & (lane < sub)
    rank = jnp.sum(jnp.where(before, jnp.broadcast_to(held_across, full), 0), axis=1, keepdims=True)
    place = (sub >> 2) * 2 + jnp.broadcast_to(rank, full)
    slot = jnp.sum(jnp.where(across == sub, place, 0), axis=0, keepdims=True)
    wanted = (jnp.broadcast_to(held_down, full) == 1) & (place == lane)
    need = jnp.sum(jnp.where(wanted, sub & 3, 0), axis=0, keepdims=True)
    slot_down = jnp.broadcast_to(slot, full).T
    last = jnp.max(jnp.where(slot_down == lane, sub, -1), axis=0, keepdims=True)
    last = jnp.where(last < 0, NONE, last)
    return slot, prev, last, need


def kernel(
    pattern_ref, expo_ref, fac, quant_hbm, out_ref,
    qraw, qs0, qs1, rowp, panel0, panel1, sums, racc, rsend, rrecv,
    xs0, xs1, zp0, zp1, cs0, cs1, cr0, cr1, co0, co1, zs0, zs1, zr0, zr1, zown,
    idxv, idxs, nrv, nrs,
    *rest,
):
    zb = (rest[0:8], rest[8:16])
    xd = (rest[16:19], rest[19:22])
    qsem, isem, send_sem, recv_sem = rest[22:]
    qs, panel, xs, zp = (qs0, qs1), (panel0, panel1), (xs0, xs1), (zp0, zp1)
    cs, cr, co, zs, zr = (cs0, cs1), (cr0, cr1), (co0, co1), (zs0, zs1), (zr0, zr1)
    w = lax.axis_index("wide")
    n = lax.axis_index("narrow")
    x, z = lax.rem(w, NX), lax.div(w, NX)
    y, c = lax.div(n, NC), lax.rem(n, NC)

    def x_peer(dx):
        return (z * NX + lax.rem(x + dx, NX), n)

    def z_peer(dz):
        return (lax.rem(z + dz, NZ) * NX + x, n)

    narrow_steps = [(dy, dc) for dy in range(NY) for dc in range(NC) if (dy, dc) != (0, 0)]

    def n_peer(dy, dc):
        return lax.rem(y + dy, NY) * NC + lax.rem(c + dc, NC)

    barrier = pltpu.get_barrier_semaphore()
    peers = [x_peer(d) for d in range(1, NX)] + [z_peer(d) for d in range(1, NZ)]
    peers += [(w, n_peer(*s)) for s in narrow_steps]
    for peer in peers:
        pl.semaphore_signal(barrier, inc=1, device_id=peer, device_id_type=MESH)

    fetch = pltpu.make_async_copy(quant_hbm, qraw, qsem)
    fetch.start()

    for k in range(BLK):
        block = fac[k * TILE : (k + 1) * TILE, :].astype(BF)
        rowp[n * BLK + k] = block
        zb[0][0][k] = block[:HALF]
        zb[1][0][k] = block[HALF:]
    idxv[...] = jnp.zeros((8, TILE), jnp.int32)
    idxv[0:4, 0:GROUP] = pattern_ref[...]
    rows = index_rows(idxv[...].T[:GROUP, :4])
    for i, row in enumerate(rows):
        idxv[i : i + 1, :] = row
    spill = pltpu.make_async_copy(idxv, idxs, isem.at[0])
    spill.start()
    sums[NONE] = jnp.zeros((HALF, RANK), F32)

    pl.semaphore_wait(barrier, len(peers))
    sent = []
    used = iter(range(MESSAGES))

    def send(src, dst, peer):
        i = next(used)
        copy = pltpu.make_async_remote_copy(
            src_ref=src, dst_ref=dst, send_sem=send_sem.at[i], recv_sem=recv_sem.at[i],
            device_id=peer, device_id_type=MESH,
        )
        copy.start()
        sent.append(copy)
        return copy

    def settle():
        while sent:
            sent.pop().wait_send()

    ring = {}

    def ring_send(h, r):
        up_src, up_dst = zb[h][(1 - r) % NZ], zb[h][(-r) % NZ]
        down_src, down_dst = zb[h][r - 1], zb[h][r]
        if r == 4:
            up_src, up_dst = up_src.at[pl.ds(0, 2)], up_dst.at[pl.ds(0, 2)]
            down_src, down_dst = down_src.at[pl.ds(2, 2)], down_dst.at[pl.ds(2, 2)]
        ring[h, r] = (send(up_src, up_dst, z_peer(1)), send(down_src, down_dst, z_peer(NZ - 1)))

    dense = {}

    def dense_send(h):
        for dx in (2, 1, 3):
            dense[h, dx] = send(zb[h][0], xd[h][dx - 1], x_peer(dx))

    needs, of_x, of_z = [], {}, {}
    for dx in range(1, NX):
        of_x[NX - dx] = len(needs)
        needs.append(send(idxv, nrv.at[len(needs)], x_peer(dx)))
    for dz in NEAR_Z:
        of_z[NZ - dz] = len(needs)
        needs.append(send(idxv, nrv.at[len(needs)], z_peer(dz)))
    ring_send(0, 1)
    dense_send(0)
    mine = rowp.at[pl.ds(n * BLK, BLK)]
    row_in = [send(mine, mine, (w, n_peer(*s))) for s in narrow_steps]

    def owner(d, dx=0):
        return lax.rem(z + d, NZ) * NX + lax.rem(x + dx, NX)

    panel_in = {0: [], 1: []}

    def keep(h, source, at):
        for r in range(2):
            panel[h][at + r] = source[idxs[3, at + r]]

    def spread_along_z(h):
        place = 0
        for dx in (2, 1, 3):
            dense[h, dx].wait_recv()
            source = xd[h][dx - 1]
            at = owner(0, NX - dx) * 2
            for dz in NEAR_Z:
                if NZ - dz not in OVER_Z[dx]:
                    continue
                for r in range(2):
                    zp[h][place, r] = source[nrs[of_z[dz], 3, at + r]]
                panel_in[h].append(send(zp[h].at[place], panel[h].at[pl.ds(at, 2)], z_peer(dz)))
                place += 1
            keep(h, source, at)

    places = {0: 0, 1: 0}

    def spread_along_x(h, d):
        source = zb[h][d]
        at = owner(d) * 2
        for dx in (2, 1, 3):
            if d == 0 or d in OVER_Z[dx]:
                continue
            for r in range(2):
                xs[h][places[h], r] = source[nrs[of_x[dx], 3, at + r]]
            panel_in[h].append(send(xs[h].at[places[h]], panel[h].at[pl.ds(at, 2)], x_peer(dx)))
            places[h] += 1
        keep(h, source, at)

    spill.wait()
    for copy in needs:
        copy.wait_recv()
    spill = pltpu.make_async_copy(nrv, nrs, isem.at[1])
    spill.start()
    spill.wait()

    for h in range(2):
        for r in range(1, 5):
            for copy in ring[h, r]:
                copy.wait_recv()
            if r < 4:
                ring_send(h, r + 1)
            if r == RING1 and h == 0:
                ring_send(1, 1)
            spread_along_x(h, (-r) % NZ)
            if r < 4:
                spread_along_x(h, r)
            if r == DENSE1 and h == 0:
                dense_send(1)
            if r == ZS and r < 4:
                spread_along_z(h)
        spread_along_x(h, 0)
        if ZS == 4:
            spread_along_z(h)

    fetch.wait()
    low = lax.broadcasted_iota(jnp.int32, (TILE, TILE), 1) < HALF

    def scale_row(b, carry):
        for pair in range(2):
            parts = []
            for t in (2 * pair, 2 * pair + 1):
                grow = lax.shift_left(1, expo_ref[t, b] + 3).astype(F32) * 0.125
                parts.append(qraw[b, 0, t].astype(F32) * grow)
            first, second = parts
            qs0[b, pair] = jnp.where(low, first, pltpu.roll(second, HALF, 1)).astype(BF)
            qs1[b, pair] = jnp.where(low, pltpu.roll(first, HALF, 1), second).astype(BF)
        return carry

    lax.fori_loop(0, GROUP, scale_row, 0)

    for copy in row_in:
        copy.wait_recv()

    def compute(h, low_row, high_row):
        def step(b, carry):
            mine = rowp[b]
            cols = jnp.concatenate([panel[h][idxs[0, b * 4 + t]] for t in range(4)], axis=0)
            pred = lax.dot_general(mine, cols, (((1,), (1,)), ((), ())), preferred_element_type=F32)
            scaled = jnp.concatenate([qs[h][b, 0], qs[h][b, 1]], axis=1).astype(F32)
            misfit = (pred - scaled).astype(BF)
            row = jnp.dot(misfit, cols, preferred_element_type=F32)
            if h == 0:
                racc[b] = row
            else:
                row = row + racc[b]
                racc[b] = row
                rsend[b] = row.astype(BF)
            term = lax.dot_general(misfit, mine, (((0,), (0,)), ((), ())), preferred_element_type=F32)
            for t in range(4):
                i = b * 4 + t
                sums[i] = term[t * HALF : (t + 1) * HALF] + sums[idxs[1, i]]
            return carry

        lax.fori_loop(low_row, high_row, step, 0, unroll=4)

    terms_in = {}

    def send_terms(h):
        for d in FAR_FIRST:
            for dx in (2, 1, 3):
                at = owner(d, dx) * 2
                for r in range(2):
                    cs[h][dx - 1, d, r] = sums[idxs[2, at + r]].astype(BF)
                terms_in[h, d, dx] = send(cs[h].at[dx - 1, d], cr[h].at[dx - 1, d], x_peer(dx))
            at = owner(d) * 2
            for r in range(2):
                co[h][d, r] = sums[idxs[2, at + r]]

    z_in = {0: [], 1: []}

    def add_terms(h, d):
        for dx in range(1, NX):
            terms_in[h, d, dx].wait_recv()
        at = owner(d) * 2
        marks = []
        for source in range(4):
            for r in range(2):
                place = idxs[3, at + r] if source == 0 else nrs[of_x[NX - source], 3, at + r]
                marks.append([jnp.where(place == k, 1.0, 0.0).astype(F32) for k in range(BLK)])

        def strip(i, carry):
            span = pl.ds(pl.multiple_of(i * 16, 16), 16)
            terms = [co[h][d, r, span, :] for r in range(2)]
            terms += [cr[h][source, d, r, span, :].astype(F32) for source in range(3) for r in range(2)]
            for k in range(BLK):
                total = terms[0] * marks[0][k]
                for term, mark in zip(terms[1:], marks[1:]):
                    total = total + term * mark[k]
                if d == 0:
                    zown[h, k, span, :] = total
                else:
                    zs[h][d - 1, k, span, :] = total.astype(BF)
            return carry

        lax.fori_loop(0, HALF // 16, strip, 0)
        if d != 0:
            z_in[h].append(send(zs[h].at[d - 1], zr[h].at[d - 1], z_peer(d)))

    for copy in panel_in[0]:
        copy.wait_recv()
    compute(0, 0, GROUP)
    send_terms(0)
    for copy in panel_in[1]:
        copy.wait_recv()
    early = len(FAR_FIRST) - LATE
    for part in range(4):
        compute(1, part * 8, part * 8 + 8)
        if part >= 4 - early:
            add_terms(0, FAR_FIRST[part - 4 + early])
    send_terms(1)
    r_in = [
        send(rsend.at[pl.ds(n_peer(*s) * BLK, BLK)], rrecv.at[j], (w, n_peer(*s)))
        for j, s in enumerate(narrow_steps)
    ]
    for d in FAR_FIRST[early:]:
        add_terms(0, d)
    for d in FAR_FIRST[:-3]:
        add_terms(1, d)
    for copy in r_in:
        copy.wait_recv()
    settled = sent[-3:]
    del sent[-3:]
    settle()
    sent.extend(settled)

    def base(i, carry):
        for k in range(BLK):
            inner = pl.ds(pl.multiple_of(i * 16, 16), 16)
            outer = pl.ds(pl.multiple_of(k * TILE + i * 16, 16), 16)
            total = racc[n * BLK + k, inner, :]
            for j in range(7):
                total = total + rrecv[j, k, inner, :].astype(F32)
            out_ref[outer, :] = fac[outer, :] - step_rate * total
        return carry

    lax.fori_loop(0, TILE // 16, base, 0)
    for d in FAR_FIRST[-3:]:
        add_terms(1, d)

    def finish(h):
        def strip(i, carry):
            for k in range(BLK):
                span = pl.ds(pl.multiple_of(i * 16, 16), 16)
                outer = pl.ds(pl.multiple_of(k * TILE + h * HALF + i * 16, 16), 16)
                total = zown[h, k, span, :]
                for j in range(7):
                    total = total + zr[h][j, k, span, :].astype(F32)
                out_ref[outer, :] = out_ref[outer, :] - step_rate * total
            return carry

        for copy in z_in[h]:
            copy.wait_recv()
        lax.fori_loop(0, HALF // 16, strip, 0)

    finish(0)
    finish(1)
    settle()


def body(factor, quant, pattern, exponent):
    vmem = pl.BlockSpec(memory_space=pltpu.VMEM)
    smem = pl.BlockSpec(memory_space=pltpu.SMEM)
    dma = pltpu.SemaphoreType.DMA
    V = pltpu.VMEM
    scratch = [
        V((GROUP, 1, 4, TILE, TILE), BF),
        V((GROUP, 2, TILE, TILE), BF), V((GROUP, 2, TILE, TILE), BF),
        V((GROUP, TILE, RANK), BF),
        V((SLOTS, HALF, RANK), BF), V((SLOTS, HALF, RANK), BF),
        V((NONE + 1, HALF, RANK), F32),
        V((GROUP, TILE, RANK), F32),
        V((GROUP, TILE, RANK), BF),
        V((7, BLK, TILE, RANK), BF),
    ]
    scratch += [V((13, 2, HALF, RANK), BF)] * 2
    scratch += [V((8, 2, HALF, RANK), BF)] * 2
    scratch += [V((3, NZ, 2, HALF, RANK), BF)] * 4
    scratch += [V((NZ, 2, HALF, RANK), F32)] * 2
    scratch += [V((7, BLK, HALF, RANK), BF)] * 4
    scratch += [V((2, BLK, HALF, RANK), F32)]
    scratch += [
        V((8, TILE), jnp.int32), pltpu.SMEM((8, TILE), jnp.int32),
        V((7, 8, TILE), jnp.int32), pltpu.SMEM((7, 8, TILE), jnp.int32),
    ]
    scratch += [V((BLK, HALF, RANK), BF)] * 22
    scratch += [dma, dma((2,)), dma((MESSAGES,)), dma((MESSAGES,))]
    return pl.pallas_call(
        kernel,
        out_shape=jax.ShapeDtypeStruct(factor.shape, factor.dtype),
        in_specs=[vmem, smem, vmem, pl.BlockSpec(memory_space=pl.ANY)],
        out_specs=vmem,
        scratch_shapes=scratch,
        compiler_params=pltpu.CompilerParams(
            collective_id=0, has_side_effects=True, vmem_limit_bytes=58 * 1024 * 1024
        ),
        cost_estimate=pl.CostEstimate(flops=3_300_000_000, bytes_accessed=6_000_000, transcendentals=0),
        name="completion_step",
    )(pattern[:, 0, :].T, exponent[:, 0, :].T, factor, quant)


def solution(mesh):
    in_specs = (
        P(("wide", "narrow"), None),
        P("wide", "narrow", None, None, None),
        P("wide", "narrow", None),
        P("wide", "narrow", None),
    )
    out_specs = P(("wide", "narrow"), None)
    return jax.shard_map(body, mesh=mesh, in_specs=in_specs, out_specs=out_specs, check_vma=False)
```

```python
import jax
import jax.numpy as jnp
from jax import lax
from jax.experimental import pallas as pl
from jax.experimental.pallas import tpu as pltpu
from jax.sharding import PartitionSpec as P

step_rate = 0.01

MESH = pl.DeviceIdType.MESH
NX = 4
NZ = 8
NY = 4
NC = 2
BLK = 4
TILE = 128
RANK = 256
GROUP = 32
SLOTS = 64
HALF = 64
NONE = 128
FAR_FIRST = (4, 3, 5, 2, 6, 1, 7, 0)
OVER_Z = {1: (1, 7), 2: (1, 7, 2, 6), 3: (1, 7)}
NEAR_Z = (1, 7, 2, 6)
MESSAGES = 160
OVER_T = (OVER_Z, OVER_Z)
CHAIN = {4: 5, 5: 6, 6: 7, 7: 0, 3: 2, 2: 1, 1: 0}
NEXT = (CHAIN, CHAIN)
DURING = ((), (-2, -1, -3), (4, 3), ())
AFTER = (
    (1, 4), (1, 3), (0, 5), (0, 2), (1, -2), (1, -1), (1, -3), (1, 5),
    (0, 6), (0, 1), (1, 2), (1, 6), (0, 7), (1, 1), (1, 7),
)
RING1, DENSE1, ZS = 2, 4, 3
BF = jnp.bfloat16
F32 = jnp.float32


def index_rows(pattern, first):
    lane32 = lax.broadcasted_iota(jnp.int32, (GROUP, TILE), 1)
    sub32 = lax.broadcasted_iota(jnp.int32, (GROUP, TILE), 0)
    spread = jnp.zeros((GROUP, TILE), jnp.int32)
    for t in range(4):
        spread = jnp.where((lane32 & 3) == t, jnp.broadcast_to(pattern[:, t : t + 1], (GROUP, TILE)), spread)
    flat = jnp.sum(jnp.where(sub32 == (lane32 >> 2), spread, 0), axis=0, keepdims=True)
    full = (TILE, TILE)
    lane = lax.broadcasted_iota(jnp.int32, full, 1)
    sub = lax.broadcasted_iota(jnp.int32, full, 0)
    turn = (sub - first) & (TILE - 1)
    own_turn = (lane - first) & (TILE - 1)
    across = jnp.broadcast_to(flat, full)
    down = across.T
    prev = jnp.max(jnp.where((across == down) & (turn < own_turn), turn, -1), axis=0, keepdims=True)
    prev = jnp.where(prev < 0, NONE, (prev + first) & (TILE - 1))
    held_down = jnp.max(jnp.where(across == sub, 1, 0), axis=1, keepdims=True)
    held_across = jnp.max(jnp.where(down == lane, 1, 0), axis=0, keepdims=True)
    before = ((lane >> 2) == (sub >> 2)) & (lane < sub)
    rank = jnp.sum(jnp.where(before, jnp.broadcast_to(held_across, full), 0), axis=1, keepdims=True)
    place = (sub >> 2) * 2 + jnp.broadcast_to(rank, full)
    slot = jnp.sum(jnp.where(across == sub, place, 0), axis=0, keepdims=True)
    wanted = (jnp.broadcast_to(held_down, full) == 1) & (place == lane)
    need = jnp.sum(jnp.where(wanted, sub & 3, 0), axis=0, keepdims=True)
    slot_down = jnp.broadcast_to(slot, full).T
    last = jnp.max(jnp.where(slot_down == lane, turn, -1), axis=0, keepdims=True)
    last = jnp.where(last < 0, NONE, (last + first) & (TILE - 1))
    return slot, prev, last, need


def kernel(
    pattern_ref, expo_ref, fac_hbm, quant_hbm, out_ref,
    fac, qraw, qs0, qs1, rowp, panel0, panel1, sums, racc, rsend, rrecv,
    xs0, xs1, zp0, zp1, cs0, cs1, cr0, cr1, co0, co1, zs0, zs1, zr0, zr1,
    zc0, zc1, zcr0, zcr1, cd0, cd1, ds0, ds1, dr0, dr1,
    idxv, idxs, nrv, nrs,
    *rest,
):
    zb = (rest[0:8], rest[8:16])
    xd = (rest[16:19], rest[19:22])
    qsem, isem, send_sem, recv_sem = rest[22:]
    qs, panel, xs, zp = (qs0, qs1), (panel0, panel1), (xs0, xs1), (zp0, zp1)
    cs, cr, co, zs, zr = (cs0, cs1), (cr0, cr1), (co0, co1), (zs0, zs1), (zr0, zr1)
    zc, zcr, cd, ds, dr = (zc0, zc1), (zcr0, zcr1), (cd0, cd1), (ds0, ds1), (dr0, dr1)
    w = lax.axis_index("wide")
    n = lax.axis_index("narrow")
    x, z = lax.rem(w, NX), lax.div(w, NX)
    y, c = lax.div(n, NC), lax.rem(n, NC)

    def x_peer(dx):
        return (z * NX + lax.rem(x + dx, NX), n)

    def z_peer(dz):
        return (lax.rem(z + dz, NZ) * NX + x, n)

    narrow_steps = [(dy, dc) for dy in range(NY) for dc in range(NC) if (dy, dc) != (0, 0)]

    def n_peer(dy, dc):
        return lax.rem(y + dy, NY) * NC + lax.rem(c + dc, NC)

    barrier = pltpu.get_barrier_semaphore()
    peers = [x_peer(d) for d in range(1, NX)] + [z_peer(d) for d in range(1, NZ)]
    peers += [(w, n_peer(*s)) for s in narrow_steps]
    for peer in peers:
        pl.semaphore_signal(barrier, inc=1, device_id=peer, device_id_type=MESH)

    grab = pltpu.make_async_copy(fac_hbm, fac, isem.at[2])
    grab.start()
    fetch = pltpu.make_async_copy(quant_hbm, qraw, qsem)
    fetch.start()
    grab.wait()
    for k in range(BLK):
        block = fac[k * TILE : (k + 1) * TILE, :].astype(BF)
        rowp[n * BLK + k] = block
        zb[0][0][k] = block[:HALF]
        zb[1][0][k] = block[HALF:]

    first_row = lax.rem(y + 1, NY) * 8
    idxv[...] = jnp.zeros((8, TILE), jnp.int32)
    idxv[0:4, 0:GROUP] = pattern_ref[...]
    rows = index_rows(idxv[...].T[:GROUP, :4], first_row * 4)
    for i, row in enumerate(rows):
        idxv[i : i + 1, :] = row
    spill = pltpu.make_async_copy(idxv, idxs, isem.at[0])
    spill.start()
    pl.semaphore_wait(barrier, len(peers))
    sent = []
    used = iter(range(MESSAGES))

    def send(src, dst, peer):
        i = next(used)
        copy = pltpu.make_async_remote_copy(
            src_ref=src, dst_ref=dst, send_sem=send_sem.at[i], recv_sem=recv_sem.at[i],
            device_id=peer, device_id_type=MESH,
        )
        copy.start()
        sent.append(copy)
        return copy

    def settle():
        while sent:
            sent.pop().wait_send()

    ring = {}

    def ring_send(h, r):
        up_src, up_dst = zb[h][(1 - r) % NZ], zb[h][(-r) % NZ]
        down_src, down_dst = zb[h][r - 1], zb[h][r]
        if r == 4:
            up_src, up_dst = up_src.at[pl.ds(0, 2)], up_dst.at[pl.ds(0, 2)]
            down_src, down_dst = down_src.at[pl.ds(2, 2)], down_dst.at[pl.ds(2, 2)]
        ring[h, r] = (send(up_src, up_dst, z_peer(1)), send(down_src, down_dst, z_peer(NZ - 1)))

    dense = {}

    def dense_send(h):
        for dx in (2, 1, 3):
            dense[h, dx] = send(zb[h][0], xd[h][dx - 1], x_peer(dx))

    needs, of_x, of_z = [], {}, {}
    for dx in range(1, NX):
        of_x[NX - dx] = len(needs)
        needs.append(send(idxv, nrv.at[len(needs)], x_peer(dx)))
    for dz in NEAR_Z:
        of_z[NZ - dz] = len(needs)
        needs.append(send(idxv, nrv.at[len(needs)], z_peer(dz)))
    ring_send(0, 1)
    dense_send(0)
    mine = rowp.at[pl.ds(n * BLK, BLK)]
    row_in = [send(mine, mine, (w, n_peer(*s))) for s in narrow_steps]

    sums[NONE] = jnp.zeros((HALF, RANK), F32)

    def owner(d, dx=0):
        return lax.rem(z + d, NZ) * NX + lax.rem(x + dx, NX)

    panel_in = {0: [], 1: []}

    def keep(h, source, at):
        for r in range(2):
            panel[h][at + r] = source[idxs[3, at + r]]

    def spread_along_z(h):
        place = 0
        for dx in (2, 1, 3):
            dense[h, dx].wait_recv()
            source = xd[h][dx - 1]
            at = owner(0, NX - dx) * 2
            for dz in NEAR_Z:
                if NZ - dz not in OVER_Z[dx]:
                    continue
                for r in range(2):
                    zp[h][place, r] = source[nrs[of_z[dz], 3, at + r]]
                panel_in[h].append(send(zp[h].at[place], panel[h].at[pl.ds(at, 2)], z_peer(dz)))
                place += 1
            keep(h, source, at)

    places = {0: 0, 1: 0}

    def spread_along_x(h, d):
        source = zb[h][d]
        at = owner(d) * 2
        for dx in (2, 1, 3):
            if d == 0 or d in OVER_Z[dx]:
                continue
            for r in range(2):
                xs[h][places[h], r] = source[nrs[of_x[dx], 3, at + r]]
            panel_in[h].append(send(xs[h].at[places[h]], panel[h].at[pl.ds(at, 2)], x_peer(dx)))
            places[h] += 1
        keep(h, source, at)

    spill.wait()
    for copy in needs:
        copy.wait_recv()
    spill = pltpu.make_async_copy(nrv, nrs, isem.at[1])
    spill.start()
    spill.wait()

    for h in range(2):
        for r in range(1, 5):
            for copy in ring[h, r]:
                copy.wait_recv()
            if r < 4:
                ring_send(h, r + 1)
            if r == RING1 and h == 0:
                ring_send(1, 1)
            for d in ((-r) % NZ, r)[: 2 if r < 4 else 1]:
                spread_along_x(h, d)
            if r == DENSE1 and h == 0:
                dense_send(1)
            if r == ZS and r < 4:
                spread_along_z(h)
        spread_along_x(h, 0)
        if ZS == 4:
            spread_along_z(h)

    fetch.wait()
    low = lax.broadcasted_iota(jnp.int32, (TILE, TILE), 1) < HALF

    def scale_row(b, carry):
        for pair in range(2):
            parts = []
            for t in (2 * pair, 2 * pair + 1):
                grow = lax.shift_left(1, expo_ref[t, b] + 3).astype(F32) * 0.125
                parts.append(qraw[b, 0, t].astype(F32) * grow)
            first, second = parts
            qs0[b, pair] = jnp.where(low, first, pltpu.roll(second, HALF, 1)).astype(BF)
            qs1[b, pair] = jnp.where(low, pltpu.roll(first, HALF, 1), second).astype(BF)
        return carry

    lax.fori_loop(0, GROUP, scale_row, 0)

    for copy in row_in:
        copy.wait_recv()

    def compute(h, low_row, high_row):
        def step(turn, carry):
            b = lax.rem(first_row + turn, GROUP)
            mine = rowp[b]
            cols = jnp.concatenate([panel[h][idxs[0, b * 4 + t]] for t in range(4)], axis=0)
            pred = lax.dot_general(mine, cols, (((1,), (1,)), ((), ())), preferred_element_type=F32)
            scaled = jnp.concatenate([qs[h][b, 0], qs[h][b, 1]], axis=1).astype(F32)
            misfit = (pred - scaled).astype(BF)
            row = jnp.dot(misfit, cols, preferred_element_type=F32)
            if h == 0:
                racc[b] = row
            else:
                row = row + racc[b]
                racc[b] = row
                rsend[b] = row.astype(BF)
            term = lax.dot_general(misfit, mine, (((0,), (0,)), ((), ())), preferred_element_type=F32)
            for t in range(4):
                i = b * 4 + t
                sums[i] = term[t * HALF : (t + 1) * HALF] + sums[idxs[1, i]]
            return carry

        lax.fori_loop(low_row, high_row, step, 0, unroll=4)

    terms_in, near_in, dense_in, chain_in = {}, {}, {}, {}
    near = [[(dx, d) for dx in (2, 1, 3) for d in OVER_T[h][dx]] for h in range(2)]

    def send_terms(h):
        for p, (dx, d) in enumerate(near[h]):
            at = owner(d, dx) * 2
            for r in range(2):
                zc[h][p, r] = sums[idxs[2, at + r]].astype(BF)
            near_in[h, dx, d] = send(zc[h].at[p], zcr[h].at[p], z_peer(d))
        for d in FAR_FIRST:
            for dx in (2, 1, 3):
                at = owner(d, dx) * 2
                if d == 0 and OVER_T[h][dx]:
                    for r in range(2):
                        cd[h][dx - 1, r] = sums[idxs[2, at + r]]
                elif d not in OVER_T[h][dx]:
                    for r in range(2):
                        cs[h][dx - 1, d, r] = sums[idxs[2, at + r]].astype(BF)
                    terms_in[h, d, dx] = send(cs[h].at[dx - 1, d], cr[h].at[dx - 1, d], x_peer(dx))
            at = owner(d) * 2
            for r in range(2):
                co[h][d, r] = sums[idxs[2, at + r]]

    def combine(pairs, wholes, write):
        marks = [
            [[jnp.where(place == k, 1.0, 0.0).astype(F32) for k in range(BLK)] for place in places]
            for _, places in pairs
        ]

        def strip(i, carry):
            span = pl.ds(pl.multiple_of(i * 16, 16), 16)
            terms = [load(r, span).astype(F32) for load, _ in pairs for r in range(2)]
            flat = [mark for pair in marks for mark in pair]
            for k in range(BLK):
                total = terms[0] * flat[0][k]
                for term, mark in zip(terms[1:], flat[1:]):
                    total = total + term * mark[k]
                for whole in wholes:
                    total = total + whole[k, span, :].astype(F32)
                write(k, i, span, total)
            return carry

        lax.fori_loop(0, HALF // 16, strip, 0)

    def own_places(at):
        return [idxs[3, at + r] for r in range(2)]

    def peer_places(j, at):
        return [nrs[j, 3, at + r] for r in range(2)]

    def add_near(h, dx):
        if not OVER_T[h][dx]:
            return
        at = owner(0, dx) * 2
        pairs = [(lambda r, span: cd[h][dx - 1, r, span, :], own_places(at))]
        for p, (dx_p, d) in enumerate(near[h]):
            if dx_p == dx:
                near_in[h, dx, d].wait_recv()
                pairs.append(
                    (lambda r, span, p=p: zcr[h][p, r, span, :], peer_places(of_z[NZ - d], at))
                )

        def write(k, i, span, total):
            ds[h][dx - 1, k, span, :] = total.astype(BF)

        combine(pairs, [], write)
        dense_in[h, dx] = send(ds[h].at[dx - 1], dr[h].at[dx - 1], x_peer(dx))

    def add_terms(h, d):
        at = owner(d) * 2
        pairs = [(lambda r, span: co[h][d, r, span, :], own_places(at))]
        wholes = []
        for dx in range(1, NX):
            if d == 0 and OVER_T[h][dx]:
                dense_in[h, dx].wait_recv()
                wholes.append(dr[h].at[dx - 1])
            elif d not in OVER_T[h][dx]:
                terms_in[h, d, dx].wait_recv()
                pairs.append(
                    (lambda r, span, dx=dx: cr[h][dx - 1, d, r, span, :], peer_places(of_x[NX - dx], at))
                )
        for came in (e for e in FAR_FIRST if e != 0 and NEXT[h][e] == d):
            chain_in[h, came].wait_recv()
            wholes.append(zr[h].at[came - 1])

        def write(k, i, span, total):
            if d == 0:
                outer = pl.ds(pl.multiple_of(k * TILE + h * HALF + i * 16, 16), 16)
                out_ref[outer, :] = out_ref[outer, :] - step_rate * total
            else:
                zs[h][d - 1, k, span, :] = total.astype(BF)

        combine(pairs, wholes, write)
        if d != 0:
            chain_in[h, d] = send(zs[h].at[d - 1], zr[h].at[d - 1], z_peer((d - NEXT[h][d]) % NZ))

    r_in = []

    def send_rows(dy):
        for c_step in range(NC):
            if (dy, c_step) != (0, 0):
                j = narrow_steps.index((dy, c_step))
                peer = n_peer(dy, c_step)
                r_in.append(send(rsend.at[pl.ds(peer * BLK, BLK)], rrecv.at[j], (w, peer)))

    for copy in panel_in[0]:
        copy.wait_recv()
    compute(0, 0, GROUP)
    send_terms(0)
    for copy in panel_in[1]:
        copy.wait_recv()
    for part in range(4):
        compute(1, part * 8, part * 8 + 8)
        send_rows((part + 1) % NY)
        for job in DURING[part]:
            add_near(0, -job) if job < 0 else add_terms(0, job)
    send_terms(1)
    for h, job in AFTER:
        add_near(h, -job) if job < 0 else add_terms(h, job)
    for copy in r_in:
        copy.wait_recv()

    def base(i, carry):
        for k in range(BLK):
            inner = pl.ds(pl.multiple_of(i * 16, 16), 16)
            outer = pl.ds(pl.multiple_of(k * TILE + i * 16, 16), 16)
            total = racc[n * BLK + k, inner, :]
            for j in range(7):
                total = total + rrecv[j, k, inner, :].astype(F32)
            out_ref[outer, :] = fac[outer, :] - step_rate * total
        return carry

    lax.fori_loop(0, TILE // 16, base, 0)
    add_terms(0, 0)
    add_terms(1, 0)
    settle()


def body(factor, quant, pattern, exponent):
    vmem = pl.BlockSpec(memory_space=pltpu.VMEM)
    smem = pl.BlockSpec(memory_space=pltpu.SMEM)
    dma = pltpu.SemaphoreType.DMA
    V = pltpu.VMEM
    scratch = [
        V(factor.shape, F32),
        V((GROUP, 1, 4, TILE, TILE), BF),
        V((GROUP, 2, TILE, TILE), BF), V((GROUP, 2, TILE, TILE), BF),
        V((GROUP, TILE, RANK), BF),
        V((SLOTS, HALF, RANK), BF), V((SLOTS, HALF, RANK), BF),
        V((NONE + 1, HALF, RANK), F32),
        V((GROUP, TILE, RANK), F32),
        V((GROUP, TILE, RANK), BF),
        V((7, BLK, TILE, RANK), BF),
    ]
    scratch += [V((13, 2, HALF, RANK), BF)] * 2
    scratch += [V((8, 2, HALF, RANK), BF)] * 2
    scratch += [V((3, NZ, 2, HALF, RANK), BF)] * 4
    scratch += [V((NZ, 2, HALF, RANK), F32)] * 2
    scratch += [V((7, BLK, HALF, RANK), BF)] * 4
    scratch += [V((8, 2, HALF, RANK), BF)] * 4
    scratch += [V((3, 2, HALF, RANK), F32)] * 2
    scratch += [V((3, BLK, HALF, RANK), BF)] * 4
    scratch += [
        V((8, TILE), jnp.int32), pltpu.SMEM((8, TILE), jnp.int32),
        V((7, 8, TILE), jnp.int32), pltpu.SMEM((7, 8, TILE), jnp.int32),
    ]
    scratch += [V((BLK, HALF, RANK), BF)] * 22
    scratch += [dma, dma((3,)), dma((MESSAGES,)), dma((MESSAGES,))]
    return pl.pallas_call(
        kernel,
        out_shape=jax.ShapeDtypeStruct(factor.shape, factor.dtype),
        in_specs=[vmem, smem, pl.BlockSpec(memory_space=pl.ANY), pl.BlockSpec(memory_space=pl.ANY)],
        out_specs=vmem,
        scratch_shapes=scratch,
        compiler_params=pltpu.CompilerParams(
            collective_id=0, has_side_effects=True, vmem_limit_bytes=58 * 1024 * 1024
        ),
        cost_estimate=pl.CostEstimate(flops=3_300_000_000, bytes_accessed=6_000_000, transcendentals=0),
        name="completion_step",
    )(pattern[:, 0, :].T, exponent[:, 0, :].T, factor, quant)


def solution(mesh):
    in_specs = (
        P(("wide", "narrow"), None),
        P("wide", "narrow", None, None, None),
        P("wide", "narrow", None),
        P("wide", "narrow", None),
    )
    out_specs = P(("wide", "narrow"), None)
    return jax.shard_map(body, mesh=mesh, in_specs=in_specs, out_specs=out_specs, check_vma=False)
```

```python
import jax
import jax.numpy as jnp
from jax import lax
from jax.experimental import pallas as pl
from jax.experimental.pallas import tpu as pltpu
from jax.sharding import PartitionSpec as P

step_rate = 0.01

MESH = pl.DeviceIdType.MESH
NX = 4
NZ = 8
NY = 4
NC = 2
BLK = 4
TILE = 128
RANK = 256
GROUP = 32
SLOTS = 64
HALF = 64
NONE = 128
FAR_FIRST = (4, 3, 5, 2, 6, 1, 7, 0)
OVER_Z = {1: (1, 7), 2: (1, 7, 2, 6), 3: (1, 7)}
NEAR_Z = (1, 7, 2, 6)
MESSAGES = 160
OVER_T = (OVER_Z, OVER_Z)
CHAIN = {4: 5, 5: 6, 6: 7, 7: 0, 3: 2, 2: 1, 1: 0}
NEXT = (CHAIN, CHAIN)
AFTER = (
    (0, 4), (0, 3), (0, -2), (0, -1), (0, -3), (1, 4), (1, 3), (0, 5), (0, 2), (1, -2), (1, -1), (1, -3),
    (1, 5), (0, 6), (0, 1), (1, 2), (1, 6), (0, 7), (1, 1), (1, 7),
)
RING1, DENSE1, ZS = 2, 4, 3
BF = jnp.bfloat16
F32 = jnp.float32


def index_rows(pattern, first):
    lane32 = lax.broadcasted_iota(jnp.int32, (GROUP, TILE), 1)
    sub32 = lax.broadcasted_iota(jnp.int32, (GROUP, TILE), 0)
    spread = jnp.zeros((GROUP, TILE), jnp.int32)
    for t in range(4):
        spread = jnp.where((lane32 & 3) == t, jnp.broadcast_to(pattern[:, t : t + 1], (GROUP, TILE)), spread)
    flat = jnp.sum(jnp.where(sub32 == (lane32 >> 2), spread, 0), axis=0, keepdims=True)
    full = (TILE, TILE)
    lane = lax.broadcasted_iota(jnp.int32, full, 1)
    sub = lax.broadcasted_iota(jnp.int32, full, 0)
    turn = (sub - first) & (TILE - 1)
    own_turn = (lane - first) & (TILE - 1)
    across = jnp.broadcast_to(flat, full)
    down = across.T
    prev = jnp.max(jnp.where((across == down) & (turn < own_turn), turn, -1), axis=0, keepdims=True)
    prev = jnp.where(prev < 0, NONE, (prev + first) & (TILE - 1))
    held_down = jnp.max(jnp.where(across == sub, 1, 0), axis=1, keepdims=True)
    held_across = jnp.max(jnp.where(down == lane, 1, 0), axis=0, keepdims=True)
    before = ((lane >> 2) == (sub >> 2)) & (lane < sub)
    rank = jnp.sum(jnp.where(before, jnp.broadcast_to(held_across, full), 0), axis=1, keepdims=True)
    place = (sub >> 2) * 2 + jnp.broadcast_to(rank, full)
    slot = jnp.sum(jnp.where(across == sub, place, 0), axis=0, keepdims=True)
    wanted = (jnp.broadcast_to(held_down, full) == 1) & (place == lane)
    need = jnp.sum(jnp.where(wanted, sub & 3, 0), axis=0, keepdims=True)
    slot_down = jnp.broadcast_to(slot, full).T
    last = jnp.max(jnp.where(slot_down == lane, turn, -1), axis=0, keepdims=True)
    last = jnp.where(last < 0, NONE, (last + first) & (TILE - 1))
    return slot, prev, last, need


def kernel(
    pattern_ref, expo_ref, fac_hbm, quant_hbm, out_ref,
    fac, qraw, qs0, qs1, rowp, panel0, panel1, sums, racc, rsend, rrecv,
    xs0, xs1, zp0, zp1, cs0, cs1, cr0, cr1, co0, co1, zs0, zs1, zr0, zr1,
    zc0, zc1, zcr0, zcr1, cd0, cd1, ds0, ds1, dr0, dr1,
    idxv, idxs, nrv, nrs,
    *rest,
):
    zb = (rest[0:8], rest[8:16])
    xd = (rest[16:19], rest[19:22])
    qsem, isem, send_sem, recv_sem = rest[22:]
    qs, panel, xs, zp = (qs0, qs1), (panel0, panel1), (xs0, xs1), (zp0, zp1)
    cs, cr, co, zs, zr = (cs0, cs1), (cr0, cr1), (co0, co1), (zs0, zs1), (zr0, zr1)
    zc, zcr, cd, ds, dr = (zc0, zc1), (zcr0, zcr1), (cd0, cd1), (ds0, ds1), (dr0, dr1)
    w = lax.axis_index("wide")
    n = lax.axis_index("narrow")
    x, z = lax.rem(w, NX), lax.div(w, NX)
    y, c = lax.div(n, NC), lax.rem(n, NC)

    def x_peer(dx):
        return (z * NX + lax.rem(x + dx, NX), n)

    def z_peer(dz):
        return (lax.rem(z + dz, NZ) * NX + x, n)

    narrow_steps = [(dy, dc) for dy in range(NY) for dc in range(NC) if (dy, dc) != (0, 0)]

    def n_peer(dy, dc):
        return lax.rem(y + dy, NY) * NC + lax.rem(c + dc, NC)

    barrier = pltpu.get_barrier_semaphore()
    peers = [x_peer(d) for d in range(1, NX)] + [z_peer(d) for d in range(1, NZ)]
    peers += [(w, n_peer(*s)) for s in narrow_steps]
    for peer in peers:
        pl.semaphore_signal(barrier, inc=1, device_id=peer, device_id_type=MESH)

    grab = pltpu.make_async_copy(fac_hbm, fac, isem.at[2])
    grab.start()
    fetch = pltpu.make_async_copy(quant_hbm, qraw, qsem)
    fetch.start()
    grab.wait()
    for k in range(BLK):
        block = fac[k * TILE : (k + 1) * TILE, :].astype(BF)
        rowp[n * BLK + k] = block
        zb[0][0][k] = block[:HALF]
        zb[1][0][k] = block[HALF:]

    first_row = lax.rem(y + 1, NY) * 8
    idxv[...] = jnp.zeros((8, TILE), jnp.int32)
    idxv[0:4, 0:GROUP] = pattern_ref[...]
    rows = index_rows(idxv[...].T[:GROUP, :4], first_row * 4)
    for i, row in enumerate(rows):
        idxv[i : i + 1, :] = row
    spill = pltpu.make_async_copy(idxv, idxs, isem.at[0])
    spill.start()
    pl.semaphore_wait(barrier, len(peers))
    sent = []
    used = iter(range(MESSAGES))

    def send(src, dst, peer):
        i = next(used)
        copy = pltpu.make_async_remote_copy(
            src_ref=src, dst_ref=dst, send_sem=send_sem.at[i], recv_sem=recv_sem.at[i],
            device_id=peer, device_id_type=MESH,
        )
        copy.start()
        sent.append(copy)
        return copy

    def settle():
        while sent:
            sent.pop().wait_send()

    ring = {}

    def ring_send(h, r):
        up_src, up_dst = zb[h][(1 - r) % NZ], zb[h][(-r) % NZ]
        down_src, down_dst = zb[h][r - 1], zb[h][r]
        if r == 4:
            up_src, up_dst = up_src.at[pl.ds(0, 2)], up_dst.at[pl.ds(0, 2)]
            down_src, down_dst = down_src.at[pl.ds(2, 2)], down_dst.at[pl.ds(2, 2)]
        ring[h, r] = (send(up_src, up_dst, z_peer(1)), send(down_src, down_dst, z_peer(NZ - 1)))

    dense = {}

    def dense_send(h):
        for dx in (2, 1, 3):
            dense[h, dx] = send(zb[h][0], xd[h][dx - 1], x_peer(dx))

    needs, of_x, of_z = [], {}, {}
    for dx in range(1, NX):
        of_x[NX - dx] = len(needs)
        needs.append(send(idxv, nrv.at[len(needs)], x_peer(dx)))
    for dz in NEAR_Z:
        of_z[NZ - dz] = len(needs)
        needs.append(send(idxv, nrv.at[len(needs)], z_peer(dz)))
    ring_send(0, 1)
    dense_send(0)
    mine = rowp.at[pl.ds(n * BLK, BLK)]
    row_in = [send(mine, mine, (w, n_peer(*s))) for s in narrow_steps]

    sums[NONE] = jnp.zeros((HALF, RANK), F32)

    def owner(d, dx=0):
        return lax.rem(z + d, NZ) * NX + lax.rem(x + dx, NX)

    panel_in = {0: [], 1: []}

    def keep(h, source, at):
        for r in range(2):
            panel[h][at + r] = source[idxs[3, at + r]]

    def spread_along_z(h):
        place = 0
        for dx in (2, 1, 3):
            dense[h, dx].wait_recv()
            source = xd[h][dx - 1]
            at = owner(0, NX - dx) * 2
            for dz in NEAR_Z:
                if NZ - dz not in OVER_Z[dx]:
                    continue
                for r in range(2):
                    zp[h][place, r] = source[nrs[of_z[dz], 3, at + r]]
                panel_in[h].append(send(zp[h].at[place], panel[h].at[pl.ds(at, 2)], z_peer(dz)))
                place += 1
            keep(h, source, at)

    places = {0: 0, 1: 0}

    def spread_along_x(h, d):
        source = zb[h][d]
        at = owner(d) * 2
        for dx in (2, 1, 3):
            if d == 0 or d in OVER_Z[dx]:
                continue
            for r in range(2):
                xs[h][places[h], r] = source[nrs[of_x[dx], 3, at + r]]
            panel_in[h].append(send(xs[h].at[places[h]], panel[h].at[pl.ds(at, 2)], x_peer(dx)))
            places[h] += 1
        keep(h, source, at)

    spill.wait()
    for copy in needs:
        copy.wait_recv()
    spill = pltpu.make_async_copy(nrv, nrs, isem.at[1])
    spill.start()
    spill.wait()

    for h in range(2):
        for r in range(1, 5):
            for copy in ring[h, r]:
                copy.wait_recv()
            if r < 4:
                ring_send(h, r + 1)
            if r == RING1 and h == 0:
                ring_send(1, 1)
            for d in ((-r) % NZ, r)[: 2 if r < 4 else 1]:
                spread_along_x(h, d)
            if r == DENSE1 and h == 0:
                dense_send(1)
            if r == ZS and r < 4:
                spread_along_z(h)
        spread_along_x(h, 0)
        if ZS == 4:
            spread_along_z(h)

    fetch.wait()
    low = lax.broadcasted_iota(jnp.int32, (TILE, TILE), 1) < HALF

    def scale_row(b, carry):
        for pair in range(2):
            parts = []
            for t in (2 * pair, 2 * pair + 1):
                grow = lax.shift_left(1, expo_ref[t, b] + 3).astype(F32) * 0.125
                parts.append(qraw[b, 0, t].astype(F32) * grow)
            first, second = parts
            qs0[b, pair] = jnp.where(low, first, pltpu.roll(second, HALF, 1)).astype(BF)
            qs1[b, pair] = jnp.where(low, pltpu.roll(first, HALF, 1), second).astype(BF)
        return carry

    lax.fori_loop(0, GROUP, scale_row, 0)

    for copy in row_in:
        copy.wait_recv()

    def compute(h, low_row, high_row):
        def step(turn, carry):
            b = lax.rem(first_row + turn, GROUP)
            mine = rowp[b]
            cols = jnp.concatenate([panel[h][idxs[0, b * 4 + t]] for t in range(4)], axis=0)
            pred = lax.dot_general(mine, cols, (((1,), (1,)), ((), ())), preferred_element_type=F32)
            scaled = jnp.concatenate([qs[h][b, 0], qs[h][b, 1]], axis=1).astype(F32)
            misfit = (pred - scaled).astype(BF)
            row = jnp.dot(misfit, cols, preferred_element_type=F32)
            if h == 0:
                racc[b] = row
            else:
                row = row + racc[b]
                racc[b] = row
                rsend[b] = row.astype(BF)
            term = lax.dot_general(misfit, mine, (((0,), (0,)), ((), ())), preferred_element_type=F32)
            for t in range(4):
                i = b * 4 + t
                sums[i] = term[t * HALF : (t + 1) * HALF] + sums[idxs[1, i]]
            return carry

        lax.fori_loop(low_row, high_row, step, 0, unroll=4)

    terms_in, near_in, dense_in, chain_in = {}, {}, {}, {}
    near = [[(dx, d) for dx in (2, 1, 3) for d in OVER_T[h][dx]] for h in range(2)]

    def send_terms(h):
        for p, (dx, d) in enumerate(near[h]):
            at = owner(d, dx) * 2
            for r in range(2):
                zc[h][p, r] = sums[idxs[2, at + r]].astype(BF)
            near_in[h, dx, d] = send(zc[h].at[p], zcr[h].at[p], z_peer(d))
        for d in FAR_FIRST:
            for dx in (2, 1, 3):
                at = owner(d, dx) * 2
                if d == 0 and OVER_T[h][dx]:
                    for r in range(2):
                        cd[h][dx - 1, r] = sums[idxs[2, at + r]]
                elif d not in OVER_T[h][dx]:
                    for r in range(2):
                        cs[h][dx - 1, d, r] = sums[idxs[2, at + r]].astype(BF)
                    terms_in[h, d, dx] = send(cs[h].at[dx - 1, d], cr[h].at[dx - 1, d], x_peer(dx))
            at = owner(d) * 2
            for r in range(2):
                co[h][d, r] = sums[idxs[2, at + r]]

    def combine(pairs, wholes, write):
        marks = [
            [[jnp.where(place == k, 1.0, 0.0).astype(F32) for k in range(BLK)] for place in places]
            for _, places in pairs
        ]

        def strip(i, carry):
            span = pl.ds(pl.multiple_of(i * 16, 16), 16)
            terms = [load(r, span).astype(F32) for load, _ in pairs for r in range(2)]
            flat = [mark for pair in marks for mark in pair]
            for k in range(BLK):
                total = terms[0] * flat[0][k]
                for term, mark in zip(terms[1:], flat[1:]):
                    total = total + term * mark[k]
                for whole in wholes:
                    total = total + whole[k, span, :].astype(F32)
                write(k, i, span, total)
            return carry

        lax.fori_loop(0, HALF // 16, strip, 0)

    def own_places(at):
        return [idxs[3, at + r] for r in range(2)]

    def peer_places(j, at):
        return [nrs[j, 3, at + r] for r in range(2)]

    def add_near(h, dx):
        if not OVER_T[h][dx]:
            return
        at = owner(0, dx) * 2
        pairs = [(lambda r, span: cd[h][dx - 1, r, span, :], own_places(at))]
        for p, (dx_p, d) in enumerate(near[h]):
            if dx_p == dx:
                near_in[h, dx, d].wait_recv()
                pairs.append(
                    (lambda r, span, p=p: zcr[h][p, r, span, :], peer_places(of_z[NZ - d], at))
                )

        def write(k, i, span, total):
            ds[h][dx - 1, k, span, :] = total.astype(BF)

        combine(pairs, [], write)
        dense_in[h, dx] = send(ds[h].at[dx - 1], dr[h].at[dx - 1], x_peer(dx))

    def add_terms(h, d):
        at = owner(d) * 2
        pairs = [(lambda r, span: co[h][d, r, span, :], own_places(at))]
        wholes = []
        for dx in range(1, NX):
            if d == 0 and OVER_T[h][dx]:
                dense_in[h, dx].wait_recv()
                wholes.append(dr[h].at[dx - 1])
            elif d not in OVER_T[h][dx]:
                terms_in[h, d, dx].wait_recv()
                pairs.append(
                    (lambda r, span, dx=dx: cr[h][dx - 1, d, r, span, :], peer_places(of_x[NX - dx], at))
                )
        for came in (e for e in FAR_FIRST if e != 0 and NEXT[h][e] == d):
            chain_in[h, came].wait_recv()
            wholes.append(zr[h].at[came - 1])

        def write(k, i, span, total):
            if d == 0:
                outer = pl.ds(pl.multiple_of(k * TILE + h * HALF + i * 16, 16), 16)
                out_ref[outer, :] = out_ref[outer, :] - step_rate * total
            else:
                zs[h][d - 1, k, span, :] = total.astype(BF)

        combine(pairs, wholes, write)
        if d != 0:
            chain_in[h, d] = send(zs[h].at[d - 1], zr[h].at[d - 1], z_peer((d - NEXT[h][d]) % NZ))

    r_in = []

    def send_rows(dy):
        for c_step in range(NC):
            if (dy, c_step) != (0, 0):
                j = narrow_steps.index((dy, c_step))
                peer = n_peer(dy, c_step)
                r_in.append(send(rsend.at[pl.ds(peer * BLK, BLK)], rrecv.at[j], (w, peer)))

    for copy in panel_in[0]:
        copy.wait_recv()
    compute(0, 0, GROUP)
    send_terms(0)
    for copy in panel_in[1]:
        copy.wait_recv()
    for part in range(4):
        compute(1, part * 8, part * 8 + 8)
        send_rows((part + 1) % NY)
    send_terms(1)
    for h, job in AFTER:
        add_near(h, -job) if job < 0 else add_terms(h, job)
    for copy in r_in:
        copy.wait_recv()

    def base(i, carry):
        for k in range(BLK):
            inner = pl.ds(pl.multiple_of(i * 16, 16), 16)
            outer = pl.ds(pl.multiple_of(k * TILE + i * 16, 16), 16)
            total = racc[n * BLK + k, inner, :]
            for j in range(7):
                total = total + rrecv[j, k, inner, :].astype(F32)
            out_ref[outer, :] = fac[outer, :] - step_rate * total
        return carry

    lax.fori_loop(0, TILE // 16, base, 0)
    add_terms(0, 0)
    add_terms(1, 0)
    settle()


def body(factor, quant, pattern, exponent):
    vmem = pl.BlockSpec(memory_space=pltpu.VMEM)
    smem = pl.BlockSpec(memory_space=pltpu.SMEM)
    dma = pltpu.SemaphoreType.DMA
    V = pltpu.VMEM
    scratch = [
        V(factor.shape, F32),
        V((GROUP, 1, 4, TILE, TILE), BF),
        V((GROUP, 2, TILE, TILE), BF), V((GROUP, 2, TILE, TILE), BF),
        V((GROUP, TILE, RANK), BF),
        V((SLOTS, HALF, RANK), BF), V((SLOTS, HALF, RANK), BF),
        V((NONE + 1, HALF, RANK), F32),
        V((GROUP, TILE, RANK), F32),
        V((GROUP, TILE, RANK), BF),
        V((7, BLK, TILE, RANK), BF),
    ]
    scratch += [V((13, 2, HALF, RANK), BF)] * 2
    scratch += [V((8, 2, HALF, RANK), BF)] * 2
    scratch += [V((3, NZ, 2, HALF, RANK), BF)] * 4
    scratch += [V((NZ, 2, HALF, RANK), F32)] * 2
    scratch += [V((7, BLK, HALF, RANK), BF)] * 4
    scratch += [V((8, 2, HALF, RANK), BF)] * 4
    scratch += [V((3, 2, HALF, RANK), F32)] * 2
    scratch += [V((3, BLK, HALF, RANK), BF)] * 4
    scratch += [
        V((8, TILE), jnp.int32), pltpu.SMEM((8, TILE), jnp.int32),
        V((7, 8, TILE), jnp.int32), pltpu.SMEM((7, 8, TILE), jnp.int32),
    ]
    scratch += [V((BLK, HALF, RANK), BF)] * 22
    scratch += [dma, dma((3,)), dma((MESSAGES,)), dma((MESSAGES,))]
    return pl.pallas_call(
        kernel,
        out_shape=jax.ShapeDtypeStruct(factor.shape, factor.dtype),
        in_specs=[vmem, smem, pl.BlockSpec(memory_space=pl.ANY), pl.BlockSpec(memory_space=pl.ANY)],
        out_specs=vmem,
        scratch_shapes=scratch,
        compiler_params=pltpu.CompilerParams(
            collective_id=0, has_side_effects=True, vmem_limit_bytes=58 * 1024 * 1024
        ),
        cost_estimate=pl.CostEstimate(flops=3_300_000_000, bytes_accessed=6_000_000, transcendentals=0),
        name="completion_step",
    )(pattern[:, 0, :].T, exponent[:, 0, :].T, factor, quant)


def solution(mesh):
    in_specs = (
        P(("wide", "narrow"), None),
        P("wide", "narrow", None, None, None),
        P("wide", "narrow", None),
        P("wide", "narrow", None),
    )
    out_specs = P(("wide", "narrow"), None)
    return jax.shard_map(body, mesh=mesh, in_specs=in_specs, out_specs=out_specs, check_vma=False)
```
